512 devices in a mesh: dp: 128 (over y, z, core), rep: 4 (over x).
Axes of the slice: x: 4, y: 4, z: 16, core: 2. Of those that a mesh axis runs over, the one named last changes fastest.
Arguments:
- q_raw: bfloat16 [3, 1536, 8192], P(None, 'dp', 'rep'), may hold values from -16 to 16
- k_raw: bfloat16 [3, 1536, 512], P(None, 'dp', 'rep'), may hold values from -8 to 8
- v_raw: bfloat16 [3, 1536, 512], P(None, 'dp', 'rep'), may hold values from -6 to 6
- q_gain: float32 [128], replicated, may hold values from 0.6 to 5.5
- k_gain: float32 [128], replicated, may hold values from 0.6 to 5.5
- kv_pool: bfloat16 [6144, 64, 2, 512], P('dp', None, None, 'rep'), may hold values from -6 to 6
- page_table: int32 [1536, 4], P('dp'), may hold values from 0 to 47, as said below
- cache_len: int32 [1536], P('dp'), may hold values from 1 to 253, as said below
- out_pages: int32 [1024], P('dp'), may hold values from 0 to 47, as said below
- in_slots: int32 [1024], P('dp'), may hold values from 0 to 47, as said below
- hidden_in: bfloat16 [3, 1536, 4096], P(None, 'dp', 'rep'), may hold values from -48 to 48
- ln_gain: float32 [4096], replicated, may hold values from 0.1 to 1.9
- route_ids: int32 [3, 1536, 8], P(None, 'dp'), may hold values from 0 to 63, all different within a row; in each aligned block of 12 rows (0 to 11, 12 to 23, ..., all dimensions but the last counted through in order) at most 2 rows name the same one
- route_logits: float32 [3, 1536, 8], P(None, 'dp'), may hold values from -4 to 4
- w_gate: bfloat16 [128, 4096, 512], P('dp', None, 'rep'), may hold values from -0.09375 to 0.09375
- w_up: bfloat16 [128, 4096, 512], P('dp', None, 'rep'), may hold values from -0.09375 to 0.09375
- w_down: bfloat16 [128, 512, 4096], P('dp', None, 'rep'), may hold values from -0.1875 to 0.1875
Outputs:
- attn_out: bfloat16 [3, 1536, 8192], P(None, 'dp', 'rep')
- moe_out: bfloat16 [3, 1536, 4096], P(None, 'dp', 'rep')
The draws below stay inside these ranges and needn't reach their ends.
Inputs may be any that keep to these rules, and one draw needn't show every extreme that they name: `route_ids`: each row names 8 different experts; in each step the 12 rows of one dp index name no expert more than 2 times, a bound that some block reaches. `page_table`: the 12 rows of one dp index hold each page number of that index once. `cache_len`: the first request holds the most. `out_pages`: the 8 entries of one dp index are different pages. `in_slots`: the 8 entries of one dp index are different pages.
All inputs are finite; a program needn't handle non-finite values.
Results may differ from the reference program's by a relative error of at most 0.008.
Values may be sent and summed in bfloat16 or wider, within the bound.
A program may use at most 64 MiB of HBM per device.

```python
import math
import jax
import jax.numpy as jnp
import numpy as np
from jax import lax

D = 4096
HEADS = 64
KV_HEADS = 4
HEAD_DIM = 128
EXPERTS = 64
TOP_K = 8
FF = 1024
STEPS = 3
REQ_DEV = 12
PAGE = 64
PAGES_REQ = 4
MIGRATE = 8
CAPACITY = 2
POOL = 48
REQUESTS = 1536
PAGES_ALL = 6144
SHARDS = 128
N_DP = 128


def key_base(key):
    return jax.random.normal(key, (STEPS, REQUESTS, KV_HEADS * HEAD_DIM), jnp.float32)


def draw_k_raw(key, part):
    base = key_base(key)
    return jnp.clip(base, -8.0, 8.0).astype(jnp.bfloat16)


def draw_q_raw(key, part):
    key = jax.random.fold_in(key, 12)
    first_key = jax.random.fold_in(key, 0)
    values = jax.random.normal(first_key, (STEPS, REQUESTS, HEADS * HEAD_DIM), jnp.float32)
    return jnp.clip(values, -16.0, 16.0).astype(jnp.bfloat16)


def draw_q_gain(key, part):
    key = jax.random.fold_in(key, 13)
    return jax.random.uniform(key, (HEAD_DIM,), jnp.float32, 0.6, 1.6)


def draw_k_gain(key, part):
    key = jax.random.fold_in(key, 14)
    return jax.random.uniform(key, (HEAD_DIM,), jnp.float32, 0.6, 1.6)


def draw_hidden_in(key, part):
    key = jax.random.fold_in(key, 15)
    first_key = jax.random.fold_in(key, 0)
    rising = 3.0 ** (jnp.arange(D, dtype=jnp.float32) / D)
    values = jax.random.normal(first_key, (STEPS, REQUESTS, D), jnp.float32) * rising
    return jnp.clip(values, -48.0, 48.0).astype(jnp.bfloat16)


def rank_orders(key):
    ranks = REQUESTS // REQ_DEV
    keys = jax.random.split(key, ranks)
    return jax.vmap(lambda single: jax.random.permutation(single, POOL))(keys).astype(jnp.int32)


def draw_page_table(key, part):
    key = jax.random.fold_in(key, 16)
    return rank_orders(key).reshape(REQUESTS, PAGES_REQ)


def draw_out_pages(key, part):
    key = jax.random.fold_in(key, 17)
    return rank_orders(key)[:, :MIGRATE].reshape(-1)


def draw_in_slots(key, part):
    key = jax.random.fold_in(key, 18)
    return rank_orders(key)[:, :MIGRATE].reshape(-1)


def draw_cache_len(key, part):
    key = jax.random.fold_in(key, 19)
    longest = PAGES_REQ * PAGE - STEPS
    lengths = jax.random.randint(key, (REQUESTS,), 1, longest + 1, jnp.int32)
    return lengths.at[0].set(longest)


def block_scale(stream_key, extent, shards, low, top_value):
    level = 1.0
    for axis_at, parts in shards:
        steps = jax.random.uniform(jax.random.fold_in(jax.random.fold_in(stream_key, 6), axis_at), (parts,), jnp.float32, low / len(shards), top_value / len(shards))
        level = level * jnp.repeat(jnp.exp(steps), extent[axis_at] // parts).reshape((-1,) + (1,) * (len(extent) - 1 - axis_at))
    return level


def deal_out(own_key, own, number, rows, number_of, top, limit, lean):
    order = jax.random.permutation(own_key, number_of)
    crowded, ordinary = shares(number_of, rows * top, limit, lean, True), shares(number_of, rows * top, limit, lean, False)
    places = jnp.arange(number_of)

    def named(tallies, offset_by):
        used = int((tallies > 0).sum())
        fixed = max(1, used // 4)
        passed = fixed + (places - fixed + offset_by * (used - fixed)) % max(1, number_of - fixed)
        return jnp.zeros((number_of,), jnp.int32).at[order[jnp.where(places < fixed, places, passed)]].set(jnp.asarray(tallies, jnp.int32))

    tallies = jnp.where(number % 4 == 0, named(crowded, number // 4), named(ordinary, number - number // 4 - 1))
    mixed = jax.random.permutation(jax.random.fold_in(own, 3), number_of)
    donor, taker = mixed[0:number_of // 2 * 2:2], mixed[1:number_of // 2 * 2:2]
    room = jnp.minimum(tallies[donor] - 1, limit - tallies[taker]) // 2
    room = jnp.where((donor == order[0]) | (taker == order[0]) | (tallies[taker] == 0), 0, jnp.maximum(room, 0))
    passed = jax.random.randint(jax.random.fold_in(own, 4), (number_of // 2,), 0, 1 << 20) % (room + 1)
    tallies = tallies.at[donor].add(-passed).at[taker].add(passed)
    labels = jnp.searchsorted(jnp.cumsum(tallies), jnp.arange(rows * top), side="right").astype(jnp.int32)
    table = labels.reshape(top, rows).T
    table = table[jax.random.permutation(jax.random.fold_in(own, 1), rows)]
    offset_by = jax.random.randint(jax.random.fold_in(own, 2), (rows, 1), 0, top)
    return jnp.take_along_axis(table, (jnp.arange(top)[None, :] + offset_by) % top, axis=1)


def shares(count, total, bound, skew, full):
    portions = [(1 << 20) // math.isqrt(rank ** skew) + 1 for rank in range(1, count + 1)]
    largest = bound if full else min(bound, max(-(-total // count), total * portions[0] // sum(portions)))
    least = 1 if total - largest >= count - 1 else 0
    counts, surplus = [largest] + [least] * (count - 1), total - largest - least * (count - 1)
    while surplus > 0:
        candidates = [i for i in range(1, count) if counts[i] < largest] or [i for i in range(1, count) if counts[i] < bound]
        whole, left = sum([portions[i] for i in candidates]), surplus
        for i in candidates:
            more = min(bound - counts[i], max(1, left * portions[i] // whole), surplus)
            counts[i] = counts[i] + more
            surplus = surplus - more
    return np.array(counts)


def gaussian(stream_key, extent, spread, limit, cuts=(), kind=jnp.bfloat16):
    drawn = spread * jax.random.normal(stream_key, extent, jnp.float32)
    if cuts:
        drawn = drawn * block_scale(stream_key, extent, cuts, -0.22, 0.18)
    return jnp.clip(drawn, -limit, limit).astype(kind)


def setup_inputs(seed: int = 0) -> dict:
    arg_keys = jax.random.split(jax.random.key(seed), 18)
    q_raw = draw_q_raw(jax.random.fold_in(arg_keys[17], 71), 0)
    k_raw = draw_k_raw(jax.random.fold_in(arg_keys[17], 71), 0)
    v_raw = gaussian(arg_keys[2], (STEPS, REQUESTS, KV_HEADS * HEAD_DIM), 1.0, 6.0, ((1, 128), (2, 4)))
    q_gain = draw_q_gain(jax.random.fold_in(arg_keys[17], 71), 0)
    k_gain = draw_k_gain(jax.random.fold_in(arg_keys[17], 71), 0)
    kv_pool = gaussian(arg_keys[5], (PAGES_ALL, PAGE, 2, KV_HEADS * HEAD_DIM), 1.0, 6.0, ((0, 128), (3, 4)))
    page_table = draw_page_table(jax.random.fold_in(arg_keys[17], 71), 0)
    cache_len = draw_cache_len(jax.random.fold_in(arg_keys[17], 71), 0)
    out_pages = draw_out_pages(jax.random.fold_in(arg_keys[17], 71), 0)
    in_slots = draw_in_slots(jax.random.fold_in(arg_keys[17], 71), 0)
    hidden_in = draw_hidden_in(jax.random.fold_in(arg_keys[17], 71), 0)
    ln_gain = jnp.clip(1.0 + 0.18 * jax.random.normal(arg_keys[11], (D,), jnp.float32), 0.1, 1.9)
    route_ids_keys = jax.random.split(jax.random.fold_in(arg_keys[12], 1), STEPS * REQUESTS // REQ_DEV)
    route_ids_turns = jax.random.permutation(jax.random.fold_in(arg_keys[12], 3), STEPS * REQUESTS // REQ_DEV)
    route_ids = jax.vmap(lambda own, number: deal_out(jax.random.fold_in(arg_keys[12], 2), own, number, REQ_DEV, EXPERTS, TOP_K, CAPACITY, 2))(route_ids_keys, route_ids_turns).reshape((STEPS, REQUESTS, TOP_K))
    route_logits = gaussian(arg_keys[13], (STEPS, REQUESTS, TOP_K), 1.0, 4.0, ((1, 128),), jnp.float32)
    w_gate = gaussian(arg_keys[14], (SHARDS, D, FF // 2), D ** -0.5, 0.09375, ((0, 128), (2, 4)))
    w_up = gaussian(arg_keys[15], (SHARDS, D, FF // 2), D ** -0.5, 0.09375, ((0, 128), (2, 4)))
    w_down = gaussian(arg_keys[16], (SHARDS, FF // 2, D), FF ** -0.5, 0.1875, ((0, 128), (2, 4)))
    return {"q_raw": q_raw, "k_raw": k_raw, "v_raw": v_raw, "q_gain": q_gain, "k_gain": k_gain, "kv_pool": kv_pool, "page_table": page_table, "cache_len": cache_len, "out_pages": out_pages, "in_slots": in_slots, "hidden_in": hidden_in, "ln_gain": ln_gain, "route_ids": route_ids, "route_logits": route_logits, "w_gate": w_gate, "w_up": w_up, "w_down": w_down}


EPS = 1e-06
THETA = 1000000.0

def head_norm(values, gain):
    mean_square = lax.optimization_barrier(jnp.mean(values * values, axis=-1, keepdims=True))
    return values * lax.rsqrt(mean_square + EPS) * gain

def rotate(values, position):
    half_dim = values.shape[-1] // 2
    exponent = jnp.arange(half_dim, dtype=jnp.float32) * (2.0 / values.shape[-1])
    frequency = THETA ** (-exponent)
    angle = position.astype(jnp.float32)[:, None] * frequency[None, :]
    cosine = jnp.cos(angle)[:, None, :]
    sine_part = jnp.sin(angle)[:, None, :]
    first_half = values[..., :half_dim]
    second_half = values[..., half_dim:]
    return jnp.concatenate([first_half * cosine - second_half * sine_part, second_half * cosine + first_half * sine_part], axis=-1)

def attend(context, lengths, queries_in, keys_in, values_in, q_gain, k_gain):
    row_count, span_len, _, kv_width = context.shape
    kv_count = kv_width // HEAD_DIM
    q_count = queries_in.shape[-1] // HEAD_DIM
    groups = q_count // kv_count
    places = jnp.arange(span_len, dtype=jnp.int32)
    scaling = 1.0 / math.sqrt(HEAD_DIM)
    results = []
    for step_index in range(STEPS):
        position = lengths + step_index
        queries = queries_in[step_index].astype(jnp.float32).reshape(row_count, q_count, HEAD_DIM)
        queries = rotate(head_norm(queries, q_gain), position).astype(jnp.bfloat16)
        new_keys = keys_in[step_index].astype(jnp.float32).reshape(row_count, kv_count, HEAD_DIM)
        new_keys = rotate(head_norm(new_keys, k_gain), position).astype(jnp.bfloat16)
        fresh_rows = jnp.stack([new_keys.reshape(row_count, kv_width), values_in[step_index]], axis=1)
        landing = (places[None, :] == position[:, None])[:, :, None, None]
        context = jnp.where(landing, fresh_rows[:, None, :, :], context)
        key_rows = context[:, :, 0, :].reshape(row_count, span_len, kv_count, HEAD_DIM).astype(jnp.float32)
        value_rows = context[:, :, 1, :].reshape(row_count, span_len, kv_count, HEAD_DIM).astype(jnp.float32)
        grouped = queries.astype(jnp.float32).reshape(row_count, kv_count, groups, HEAD_DIM)
        scores = jnp.einsum('rhgd,rshd->rhgs', grouped, key_rows) * scaling
        valid = (places[None, :] <= position[:, None])[:, None, None, :]
        scores = jnp.where(valid, scores, -1e+30)
        row_top = lax.optimization_barrier(jnp.max(scores, axis=-1, keepdims=True))
        expos = jnp.where(valid, jnp.exp(scores - row_top), 0.0)
        probs = (expos / lax.optimization_barrier(jnp.sum(expos, axis=-1, keepdims=True))).astype(jnp.bfloat16)
        mixed = jnp.einsum('rhgs,rshd->rhgd', probs.astype(jnp.float32), value_rows)
        results.append(mixed.reshape(row_count, q_count * HEAD_DIM).astype(jnp.bfloat16))
    return jnp.stack(results)

def place(route_ids):
    flat_ids = route_ids.reshape(route_ids.shape[0], -1)
    hot_table = (flat_ids[:, :, None] == jnp.arange(EXPERTS, dtype=jnp.int32)[None, None, :]).astype(jnp.int32)
    before = jnp.cumsum(hot_table, axis=1) - hot_table
    return lax.optimization_barrier(jnp.sum(before * hot_table, axis=2)).reshape(route_ids.shape)

def reference(q_raw, k_raw, v_raw, q_gain, k_gain, kv_pool, page_table, cache_len, out_pages, in_slots, hidden_in, ln_gain, route_ids, route_logits, w_gate, w_up, w_down):
    ranks = N_DP
    kv_width = kv_pool.shape[-1]
    pool = kv_pool.reshape(ranks, POOL, PAGE, 2, kv_width)
    leaving = jax.vmap(lambda pages, chosen: pages[chosen])(pool, out_pages.reshape(ranks, MIGRATE))
    arriving = jnp.roll(leaving, ranks // 2, axis=0)
    pool = jax.vmap(lambda pages, chosen, incoming: pages.at[chosen].set(incoming))(pool, in_slots.reshape(ranks, MIGRATE), arriving)

    def per_rank(array_in):
        return array_in.reshape(STEPS, ranks, REQ_DEV, -1).transpose(1, 0, 2, 3)

    def one_rank(inputs):
        pages, table, lengths, queries, new_keys, new_values = inputs
        context = pages[table].reshape(REQ_DEV, PAGES_REQ * PAGE, 2, kv_width)
        return attend(context, lengths, queries, new_keys, new_values, q_gain, k_gain)
    attended = lax.map(one_rank, (pool, page_table.reshape(ranks, REQ_DEV, PAGES_REQ), cache_len.reshape(ranks, REQ_DEV), per_rank(q_raw), per_rank(k_raw), per_rank(v_raw)))
    attn_out = attended.transpose(1, 0, 2, 3).reshape(STEPS, REQUESTS, HEADS * HEAD_DIM)
    values = hidden_in.astype(jnp.float32)
    mean_square = lax.optimization_barrier(jnp.mean(values * values, axis=-1, keepdims=True))
    normed = (values * lax.rsqrt(mean_square + EPS) * ln_gain).astype(jnp.bfloat16)
    normed_rank = per_rank(normed)
    ids_rank = per_rank(route_ids)
    slots = jax.vmap(place)(ids_rank)
    section_index = jnp.broadcast_to(jnp.arange(STEPS, dtype=jnp.int32)[:, None, None], (STEPS, REQ_DEV, TOP_K))

    def fill(normed_one, ids_one, slot_one):
        buffer = jnp.zeros((EXPERTS, STEPS, CAPACITY, D), jnp.bfloat16)
        spread_rows = jnp.broadcast_to(normed_one[:, :, None, :], (STEPS, REQ_DEV, TOP_K, D))
        return buffer.at[ids_one, section_index, slot_one].set(spread_rows)
    buffers = jax.vmap(fill)(normed_rank, ids_rank, slots)

    def expert_pass(expert):
        rows_in = buffers[:, expert].reshape(-1, D)
        outputs = []
        for half_index in range(2):
            shard = half_index * EXPERTS + expert
            gate = jnp.dot(rows_in, w_gate[shard], preferred_element_type=jnp.float32)
            upper = jnp.dot(rows_in, w_up[shard], preferred_element_type=jnp.float32)
            hidden = (jax.nn.silu(gate) * upper).astype(jnp.bfloat16)
            outputs.append(jnp.dot(hidden, w_down[shard], preferred_element_type=jnp.float32).astype(jnp.bfloat16))
        return jnp.stack(outputs)
    expert_out = lax.map(expert_pass, jnp.arange(EXPERTS, dtype=jnp.int32))
    expert_out = expert_out.reshape(EXPERTS, 2, ranks, STEPS, CAPACITY, D)

    def combine(inputs):
        rank_index, ids_one, slot_one, logits_one = inputs
        picked = expert_out[:, :, rank_index]
        first_half = picked[ids_one, 0, section_index, slot_one].astype(jnp.float32)
        second_half = picked[ids_one, 1, section_index, slot_one].astype(jnp.float32)
        weights = jax.nn.softmax(logits_one, axis=-1)
        return lax.optimization_barrier(jnp.sum(weights[..., None] * (first_half + second_half), axis=2)).astype(jnp.bfloat16)
    mixed = lax.map(combine, (jnp.arange(ranks, dtype=jnp.int32), ids_rank, slots, per_rank(route_logits)))
    moe_out = mixed.transpose(1, 0, 2, 3).reshape(STEPS, REQUESTS, D)
    return (attn_out, moe_out)
```

```python
import functools
import math

import jax
import jax.numpy as jnp
import numpy as np
from jax import lax
from jax.experimental import pallas as pl
from jax.experimental.pallas import tpu as pltpu
from jax.sharding import PartitionSpec as P

NX, NY, NZ, NC = 4, 4, 16, 2
STEPS, REQ, TOP_K = 3, 12, 8
D, HEAD_DIM = 4096, 128
EPS = 1e-06
THETA = 1000000.0

LB = 4
PACK = STEPS * LB * REQ
WIDE = D // NX // LB
GROUPS = NZ // 2
PER = 2
CHUNKS = GROUPS // PER
SLAB = LB * 2 * STEPS * 2
ROWS = SLAB // LB * NY * NC
CLASSES = 4
SEL = CLASSES * SLAB
HIDE = 128
MESH = pl.DeviceIdType.MESH
F32, BF16 = jnp.float32, jnp.bfloat16


def tables():
    spread = np.zeros((SEL, 64), np.float32)
    base = np.zeros((SEL, 128), np.float32)
    row = 0
    for cls in range(CLASSES):
        for lb in range(LB):
            for zz in range(2):
                for s in range(STEPS):
                    for slot in range(2):
                        spread[row, zz * 32 + cls * 6 + s * 2 + slot] = 1
                        base[row] = zz * PACK + s * LB * REQ + lb * REQ
                        row += 1
    peers, per = NY * NC, SLAB // LB
    perm = np.zeros((peers * SLAB, peers * SLAB), np.float32)
    for lb in range(LB):
        for q in range(peers):
            for r in range(per):
                perm[(lb * peers + q) * per + r, q * SLAB + lb * per + r] = 1
    token = np.zeros((PACK, 128), np.float32)
    for s in range(STEPS):
        for lb in range(LB):
            for i in range(REQ):
                token[(s * LB + lb) * REQ + i, s * REQ + i] = 1
    return spread, base, perm, token


def dot(a, b):
    return jnp.dot(a, b, preferred_element_type=F32)


def kernel(
    source_page, out_pages, lengths,
    scaled, squares, meta, pool, queries, fresh, cosines, sines, q_gain, k_gain,
    spread, base, perm, perm_back, token,
    w_gate, w_up, w_down,
    attn, moe,
    leave, arrive, stat, rows, metas, chosen, taken, w_in, w_out,
    part_own, part_out, part_in, hidden, back_out, back_in, total, ring_out, ring_in,
    local_sem, page_sem, stat_sem, w_sem, row_sem, meta_sem, taken_sem,
    part_sem, hidden_sem, back_sem, ring_sem,
):
    dp, x = lax.axis_index("dp"), lax.axis_index("rep")
    y, z, c = dp // (NZ * NC), (dp // NC) % NZ, dp % NC
    q = y * NC + c
    right = ((y * NZ + (z + 1) % NZ) * NC + c, x)
    left = ((y * NZ + (z + NZ - 1) % NZ) * NC + c, x)
    across = (((y + 2) % NY * NZ + z) * NC + c, x)

    def along_x(by):
        return (dp, (x + by) % NX)

    def peer(by):
        other = (q + by) % (NY * NC)
        return other, ((other // NC * NZ + z) * NC + other % NC, x)

    def send(src, dst, sem, at, device):
        return pltpu.make_async_remote_copy(
            src_ref=src, dst_ref=dst, send_sem=sem.at[(0,) + at], recv_sem=sem.at[(1,) + at],
            device_id=device, device_id_type=MESH,
        )

    page_copy = send(leave, arrive, page_sem, (), across)
    stat_copies = [send(stat.at[0], stat.at[by], stat_sem, (by,), along_x(by)) for by in (1, 2, 3)]

    def weight_copies(by):
        to = (x + by) % NX
        piece = pl.ds(to * (D // NX), D // NX)
        return [
            send(w.at[piece, :], w_in.at[by, :, pl.ds(n * HIDE, HIDE)], w_sem, (by, n), along_x(by))
            for n, w in enumerate((w_gate, w_up))
        ]

    def row_copies(g):
        out = []
        for way, device in ((0, right), (1, left)):
            src = jnp.where(g == 0, 2 * GROUPS - 1, 2 * (g - 1) + way)
            dst = 2 * g + way
            out.append(send(rows.at[src], rows.at[dst], row_sem, (g, way), device))
            out.append(send(metas.at[src], metas.at[dst], meta_sem, (g, way), device))
        return out

    def last_row_copies():
        g = GROUPS - 1
        a, b = pl.ds(0, 96), pl.ds(96, 48)
        return [
            send(rows.at[2 * g - 2, a], rows.at[2 * g, a], row_sem, (g, 0), right),
            send(rows.at[2 * g - 1, b], rows.at[2 * g, b], row_sem, (g, 1), left),
            send(metas.at[2 * g - 2], metas.at[2 * g], meta_sem, (g, 0), right),
        ]

    def taken_copy(g, by):
        other, device = peer(by)
        cls = other // NC % 2 * NC + other % NC
        return send(chosen.at[g, cls], taken.at[g, q], taken_sem, (g, by), device)

    def part_copy(ch, by):
        return send(part_out.at[ch, by], part_in.at[ch, by], part_sem, (ch, by), along_x(by))

    def hidden_copy(ch, by):
        return send(hidden.at[ch, 0], hidden.at[ch, by], hidden_sem, (ch, by), along_x(by))

    def back_copy(ch, by):
        other, device = peer(by)
        return send(back_out.at[ch, other], back_in.at[ch, q], back_sem, (ch, by), device)

    def ring_copies(j):
        return [
            send(ring_out.at[j, way], ring_in.at[j, way], ring_sem, (j, way), device)
            for way, device in ((0, right), (1, left))
        ]

    def first_ring_copies():
        a, b = pl.ds(0, 96), pl.ds(96, 48)
        return [
            send(ring_out.at[0, 0, a], ring_in.at[0, 0, a], ring_sem, (0, 0), right),
            send(ring_out.at[0, 1, b], ring_in.at[0, 1, b], ring_sem, (0, 1), left),
        ]

    own = pl.ds(x * (D // NX), D // NX)
    local = [
        pltpu.make_async_copy(w.at[own, :], w_in.at[0, :, pl.ds(n * HIDE, HIDE)], local_sem.at[n])
        for n, w in enumerate((w_gate, w_up))
    ]
    for by in range(NX):
        src = pl.ds((x + NX - by) % NX * HIDE, HIDE)
        local.append(
            pltpu.make_async_copy(w_down.at[src, :], w_out.at[pl.ds(by * HIDE, HIDE), :], local_sem.at[2 + by])
        )
    barrier = pltpu.get_barrier_semaphore()
    devices = [right, left] + [along_x(by) for by in (1, 2, 3)] + [peer(by)[1] for by in range(1, 8)]
    for device in devices:
        pl.semaphore_signal(barrier, inc=1, device_id=device, device_id_type=MESH)
    for copy in local:
        copy.start()
    stat[0] = squares[...]
    metas[2 * GROUPS - 1] = meta[...]
    ring_in[0, 0, 96:144, :] = jnp.zeros((48, WIDE), BF16)
    ring_in[0, 1, 0:96, :] = jnp.zeros((96, WIDE), BF16)
    for n in range(8):
        leave[n] = pool[out_pages[n]]
    pl.semaphore_wait(barrier, len(devices))

    for copy in stat_copies:
        copy.start()
    for by in (1, 3, 2):
        for copy in weight_copies(by):
            copy.start()

    for copy in stat_copies:
        copy.wait_recv()
    mean = (stat[0] + stat[1] + stat[2] + stat[3]) * (1.0 / D)
    scale = lax.rsqrt(mean[0:1] + EPS)
    scale = jnp.sum(token[...] * scale, axis=1, keepdims=True)
    rows[2 * GROUPS - 1] = (scaled[...] * scale).astype(BF16)
    for copy in row_copies(0):
        copy.start()
    page_copy.start()

    lane = lax.broadcasted_iota(jnp.int32, (SEL, 128), 1)

    def unpack(g):
        pair = metas[pl.ds(2 * g, 2)].reshape(64, 128)
        wide = dot(spread[...], pair)
        code = jnp.sum(jnp.where(lane == z, wide, 0.0), axis=1, keepdims=True) + base[:, 0:1]
        weight = jnp.sum(
            jnp.where((lane == z + NZ) | (lane == z + 2 * NZ), wide, 0.0), axis=1, keepdims=True
        )
        return code, weight

    def choose(g, carry):
        @pl.when(g < GROUPS - 1)
        def _():
            for copy in row_copies(g):
                copy.wait_recv()

        @pl.when(g < GROUPS - 2)
        def _():
            for copy in row_copies(g + 1):
                copy.start()

        @pl.when(g == GROUPS - 2)
        def _():
            for copy in last_row_copies():
                copy.start()

        @pl.when(g == GROUPS - 1)
        def _():
            for copy in last_row_copies():
                copy.wait_recv()

        code, _ = unpack(g)
        column = lax.broadcasted_iota(jnp.int32, (SEL, 2 * PACK), 1).astype(F32)
        hot = jnp.where(column == code, 1.0, 0.0).astype(BF16)
        picked = dot(hot, rows[pl.ds(2 * g, 2)].reshape(2 * PACK, WIDE)).astype(BF16)
        chosen[g] = picked.reshape(CLASSES, SLAB, WIDE)
        for by in range(1, 8):
            taken_copy(g, by).start()
        taken[g, q] = chosen[g, y % 2 * NC + c]
        return carry

    lax.fori_loop(0, GROUPS, choose, 0)

    for copy in local:
        copy.wait()
    for by in (1, 2, 3):
        for copy in weight_copies(by):
            copy.wait_recv()

    def first_matmul(ch):
        pieces = []
        for u in range(PER):
            g = ch * PER + u
            for by in range(1, 8):
                taken_copy(g, by).wait_recv()
            block = dot(perm[...], taken[g].reshape(NY * NC * SLAB, WIDE)).astype(BF16)
            pieces.append(
                jnp.concatenate([block[lb * ROWS : (lb + 1) * ROWS] for lb in range(LB)], axis=1)
            )
        inputs = jnp.concatenate(pieces, axis=0)
        for by in (1, 3, 2):
            part_out[ch, by] = dot(inputs, w_in[(NX - by) % NX]).astype(BF16)
            part_copy(ch, by).start()
        part_own[ch] = dot(inputs, w_in[0])

    def activate(ch):
        for by in (1, 2, 3):
            part_copy(ch, by).wait_recv()
        both = part_own[ch] + part_in[ch, 1].astype(F32) + part_in[ch, 2].astype(F32) + part_in[ch, 3].astype(F32)
        gate, upper = both[:, :HIDE], both[:, HIDE:]
        hidden[ch, 0] = (gate / (1.0 + jnp.exp(-gate)) * upper).astype(BF16)
        for by in (1, 3, 2):
            hidden_copy(ch, by).start()

    def second_matmul(ch):
        for by in (1, 2, 3):
            hidden_copy(ch, by).wait_recv()
        units = jnp.concatenate([hidden[ch, by] for by in range(NX)], axis=1)
        made = dot(units, w_out[...]).astype(BF16)
        for u in range(PER):
            part = made[u * ROWS : (u + 1) * ROWS]
            stack = jnp.concatenate([part[:, lb * WIDE : (lb + 1) * WIDE] for lb in range(LB)], axis=0)
            slabs = dot(perm_back[...], stack).astype(BF16)
            back_out[ch, :, u * SLAB : (u + 1) * SLAB, :] = slabs.reshape(NY * NC, SLAB, WIDE)
        for by in range(1, 8):
            back_copy(ch, by).start()
        back_in[ch, q] = back_out[ch, q]

    def combine(ch):
        for by in range(1, 8):
            back_copy(ch, by).wait_recv()
        for u in range(PER):
            g = ch * PER + u
            code, weight = unpack(g)
            slabs = back_in[ch, :, u * SLAB : (u + 1) * SLAB, :].astype(F32)
            both = (slabs[:CLASSES] + slabs[CLASSES:]).reshape(SEL, WIDE)
            both = (both * weight).astype(BF16)
            diagonal = lax.broadcasted_iota(jnp.int32, (SEL, SEL), 0) == lax.broadcasted_iota(
                jnp.int32, (SEL, SEL), 1
            )
            code_row = jnp.sum(jnp.where(diagonal, code, 0.0), axis=0, keepdims=True)
            place = lax.broadcasted_iota(jnp.int32, (2 * PACK, SEL), 0).astype(F32)
            hot = jnp.where(place == code_row, 1.0, 0.0).astype(BF16)
            total[g] = dot(hot, both)

    def experts(it, carry):
        @pl.when(it < CHUNKS)
        def _():
            first_matmul(it)

        @pl.when((it >= 1) & (it < CHUNKS + 1))
        def _():
            activate(it - 1)

        @pl.when((it >= 2) & (it < CHUNKS + 2))
        def _():
            second_matmul(it - 2)

        @pl.when(it >= 3)
        def _():
            combine(it - 3)

        return carry

    lax.fori_loop(0, CHUNKS + 3, experts, 0)

    scaling = 1.0 / math.sqrt(HEAD_DIM)

    def normalize(values, gain):
        mean_square = jnp.mean(values * values, axis=-1, keepdims=True)
        return values * lax.rsqrt(mean_square + EPS) * gain

    def attend(i, carry):
        pages = []
        for n in range(4):
            at = source_page[i * 4 + n]
            stayed = pool[jnp.minimum(at, 47)]
            moved = arrive[jnp.maximum(at - 48, 0)]
            pages.append(jnp.where(at < 48, stayed, moved))
        cos, sin = cosines[pl.ds(i * 16, 16)], sines[pl.ds(i * 16, 16)]
        raw = fresh[pl.ds(i * 16, 16)].astype(F32)
        keys = normalize(raw, k_gain[0:1])
        keys = keys * cos + pltpu.roll(keys, 64, axis=1) * sin
        is_key = lax.broadcasted_iota(jnp.int32, (16, 128), 0) % 2 == 0
        extra = jnp.where(is_key, keys, raw).astype(BF16)
        context = jnp.concatenate(pages + [extra, jnp.zeros((112, 128), BF16)], axis=0)
        asked = normalize(queries[pl.ds(i * 48, 48)].astype(F32), q_gain[0:1])
        cos_q = jnp.concatenate([jnp.broadcast_to(cos[2 * s : 2 * s + 1], (16, 128)) for s in range(3)], axis=0)
        sin_q = jnp.concatenate([jnp.broadcast_to(sin[2 * s : 2 * s + 1], (16, 128)) for s in range(3)], axis=0)
        asked = (asked * cos_q + pltpu.roll(asked, 64, axis=1) * sin_q).astype(BF16)
        scores = lax.dot_general(asked, context, (((1,), (1,)), ((), ())), preferred_element_type=F32) * scaling
        at = lax.broadcasted_iota(jnp.int32, (48, 640), 1)
        step = lax.broadcasted_iota(jnp.int32, (48, 640), 0) // 16
        known = at < 2 * lengths[i]
        added = (at >= 512) & (at <= 512 + 2 * step)
        valid = (known | added) & (at % 2 == 0)
        scores = jnp.where(valid, scores, -1e30)
        top = jnp.max(scores, axis=-1, keepdims=True)
        expos = jnp.where(valid, jnp.exp(scores - top), 0.0)
        probs = expos / jnp.sum(expos, axis=-1, keepdims=True)
        probs = pltpu.roll(probs, 1, axis=1).astype(BF16)
        attn[pl.ds(i * 48, 48)] = dot(probs, context).astype(BF16)
        return carry

    far = GROUPS - 1
    ring_out[0, 0] = total[far, 0:PACK].astype(BF16)
    ring_out[0, 1] = total[far, 0:PACK].astype(BF16)
    for copy in first_ring_copies():
        copy.start()
    page_copy.wait_recv()
    lax.fori_loop(0, 2, attend, 0)

    def gather_home(j, carry):
        @pl.when(j == 1)
        def _():
            for copy in first_ring_copies():
                copy.wait_recv()

        @pl.when(j > 1)
        def _():
            for copy in ring_copies(j - 1):
                copy.wait_recv()

        near = far - j
        ring_out[j, 0] = (total[near, PACK : 2 * PACK] + ring_in[j - 1, 0].astype(F32)).astype(BF16)
        ring_out[j, 1] = (total[near, 0:PACK] + ring_in[j - 1, 1].astype(F32)).astype(BF16)
        for copy in ring_copies(j):
            copy.start()

        @pl.when(j < 6)
        def _():
            lax.fori_loop(2 * j, 2 * j + 2, attend, 0)

        return carry

    lax.fori_loop(1, GROUPS, gather_home, 0)
    for copy in ring_copies(far):
        copy.wait_recv()
    moe[...] = (
        total[far, PACK : 2 * PACK] + ring_in[far, 0].astype(F32) + ring_in[far, 1].astype(F32)
    ).astype(BF16)

    page_copy.wait_send()
    for copy in stat_copies + last_row_copies() + first_ring_copies():
        copy.wait_send()
    for by in (1, 2, 3):
        for copy in weight_copies(by):
            copy.wait_send()

    def drain_pairs(g, carry):
        for by in range(1, 8):
            taken_copy(g, by).wait_send()

        @pl.when(g < GROUPS - 1)
        def _():
            for copy in row_copies(g) + ring_copies(g + 1):
                copy.wait_send()

        return carry

    def drain_chunks(ch, carry):
        for by in (1, 2, 3):
            part_copy(ch, by).wait_send()
            hidden_copy(ch, by).wait_send()
        for by in range(1, 8):
            back_copy(ch, by).wait_send()
        return carry

    lax.fori_loop(0, GROUPS, drain_pairs, 0)
    lax.fori_loop(0, CHUNKS, drain_chunks, 0)


def routing(route_ids, route_logits):
    ids = route_ids.reshape(STEPS, REQ * TOP_K)
    order = jnp.arange(REQ * TOP_K, dtype=jnp.int32)
    earlier = (ids[:, :, None] == ids[:, None, :]) & (order[None, :] < order[:, None])
    slots = jnp.sum(earlier.astype(jnp.int32), axis=2)
    target = ids * 2 + slots
    hit = target[:, :, None] == jnp.arange(128, dtype=jnp.int32)
    row = (order // TOP_K + 1)[None, :, None]
    index = jnp.sum(jnp.where(hit, row, 0), axis=1)
    index = jnp.where(index > 0, index - 1, 512).astype(F32)
    weights = jax.nn.softmax(route_logits, axis=-1).reshape(STEPS, REQ * TOP_K)
    weight = jnp.sum(jnp.where(hit, weights[:, :, None], 0.0), axis=1)
    high = lax.reduce_precision(weight, 8, 7)
    both = jnp.stack([index, high, weight - high])
    both = both.reshape(3, STEPS, 2, NZ, NC, 2).transpose(2, 4, 1, 5, 0, 3).reshape(24, 3 * NZ)
    return jnp.pad(both, ((0, 8), (0, 128 - 3 * NZ))).astype(BF16)


def local(
    q_raw, k_raw, v_raw, q_gain, k_gain, kv_pool, page_table, cache_len, out_pages, in_slots,
    hidden_in, ln_gain, route_ids, route_logits, w_gate, w_up, w_down,
):
    x = lax.axis_index("rep")
    spread, base, perm, token = tables()
    flat = page_table.reshape(-1)
    match = flat[:, None] == in_slots[None, :]
    source = jnp.where(
        jnp.any(match, axis=1), 48 + jnp.sum(jnp.where(match, jnp.arange(8, dtype=jnp.int32), 0), axis=1), flat
    )
    values = hidden_in.astype(F32)
    gain = lax.dynamic_slice(ln_gain, (x * (D // NX),), (D // NX,))
    scaled = (values * gain).reshape(STEPS, REQ, LB, WIDE).transpose(0, 2, 1, 3).reshape(PACK, WIDE)
    squares = jnp.sum(values * values, axis=-1).reshape(1, STEPS * REQ)
    squares = jnp.broadcast_to(jnp.pad(squares, ((0, 0), (0, 128 - STEPS * REQ))), (8, 128))
    meta = routing(route_ids, route_logits)
    pool = kv_pool.reshape(48, 128, HEAD_DIM)
    queries = q_raw.reshape(STEPS, REQ, 16, HEAD_DIM).transpose(1, 0, 2, 3).reshape(REQ * 48, HEAD_DIM)
    fresh = jnp.stack([k_raw, v_raw], axis=2).transpose(1, 0, 2, 3).reshape(REQ, 6, HEAD_DIM)
    fresh = jnp.pad(fresh, ((0, 0), (0, 10), (0, 0))).reshape(REQ * 16, HEAD_DIM)
    exponent = jnp.arange(HEAD_DIM // 2, dtype=F32) * (2.0 / HEAD_DIM)
    frequency = THETA ** (-exponent)
    place = jnp.arange(16, dtype=jnp.int32) // 2
    position = (cache_len[:, None] + place[None, :]).astype(F32).reshape(-1)
    angle = position[:, None] * frequency[None, :]
    cosine, sine = jnp.cos(angle), jnp.sin(angle)
    cosines = jnp.concatenate([cosine, cosine], axis=1)
    sines = jnp.concatenate([-sine, sine], axis=1)
    rows_of = lambda g: jnp.broadcast_to(g[None, :], (8, HEAD_DIM))

    smem = pl.BlockSpec(memory_space=pltpu.SMEM)
    vmem = pl.BlockSpec(memory_space=pltpu.VMEM)
    anywhere = pl.BlockSpec(memory_space=pl.ANY)
    peers = NY * NC
    sem = pltpu.SemaphoreType.DMA
    attn, moe = pl.pallas_call(
        kernel,
        out_shape=(
            jax.ShapeDtypeStruct((REQ * 48, HEAD_DIM), BF16),
            jax.ShapeDtypeStruct((PACK, WIDE), BF16),
        ),
        in_specs=[smem] * 3 + [vmem] * 15 + [anywhere] * 3,
        out_specs=(vmem, vmem),
        scratch_shapes=[
            pltpu.VMEM((8, 128, HEAD_DIM), BF16),
            pltpu.VMEM((8, 128, HEAD_DIM), BF16),
            pltpu.VMEM((NX, 8, 128), F32),
            pltpu.VMEM((NZ, PACK, WIDE), BF16),
            pltpu.VMEM((NZ, 32, 128), BF16),
            pltpu.VMEM((GROUPS, CLASSES, SLAB, WIDE), BF16),
            pltpu.VMEM((GROUPS, peers, SLAB, WIDE), BF16),
            pltpu.VMEM((NX, D // NX, 2 * HIDE), BF16),
            pltpu.VMEM((NX * HIDE, D // NX), BF16),
            pltpu.VMEM((CHUNKS, PER * ROWS, 2 * HIDE), F32),
            pltpu.VMEM((CHUNKS, NX, PER * ROWS, 2 * HIDE), BF16),
            pltpu.VMEM((CHUNKS, NX, PER * ROWS, 2 * HIDE), BF16),
            pltpu.VMEM((CHUNKS, NX, PER * ROWS, HIDE), BF16),
            pltpu.VMEM((CHUNKS, peers, PER * SLAB, WIDE), BF16),
            pltpu.VMEM((CHUNKS, peers, PER * SLAB, WIDE), BF16),
            pltpu.VMEM((GROUPS, 2 * PACK, WIDE), F32),
            pltpu.VMEM((GROUPS, 2, PACK, WIDE), BF16),
            pltpu.VMEM((GROUPS, 2, PACK, WIDE), BF16),
            sem((6,)),
            sem((2,)),
            sem((2, NX)),
            sem((2, NX, 2)),
            sem((2, GROUPS, 2)),
            sem((2, GROUPS, 2)),
            sem((2, GROUPS, peers)),
            sem((2, CHUNKS, NX)),
            sem((2, CHUNKS, NX)),
            sem((2, CHUNKS, peers)),
            sem((2, GROUPS, 2)),
        ],
        compiler_params=pltpu.CompilerParams(
            collective_id=0, has_side_effects=True, vmem_limit_bytes=48 * 1024 * 1024
        ),
    )(
        source, out_pages, cache_len,
        scaled, squares, meta, pool, queries, fresh, cosines, sines, rows_of(q_gain), rows_of(k_gain),
        jnp.asarray(spread, BF16), jnp.asarray(base), jnp.asarray(perm, BF16), jnp.asarray(perm.T, BF16),
        jnp.asarray(token),
        w_gate.reshape(D, HIDE), w_up.reshape(D, HIDE), w_down.reshape(NX * HIDE, D // NX),
    )
    attn = attn.reshape(REQ, STEPS, 16, HEAD_DIM).transpose(1, 0, 2, 3).reshape(STEPS, REQ, 16 * HEAD_DIM)
    moe = moe.reshape(STEPS, LB, REQ, WIDE).transpose(0, 2, 1, 3).reshape(STEPS, REQ, D // NX)
    return attn, moe


def solution(mesh):
    return jax.shard_map(
        local,
        mesh=mesh,
        in_specs=(
            P(None, "dp", "rep"),
            P(None, "dp", "rep"),
            P(None, "dp", "rep"),
            P(),
            P(),
            P("dp", None, None, "rep"),
            P("dp", None),
            P("dp"),
            P("dp"),
            P("dp"),
            P(None, "dp", "rep"),
            P(),
            P(None, "dp", None),
            P(None, "dp", None),
            P("dp", None, "rep"),
            P("dp", None, "rep"),
            P("dp", None, "rep"),
        ),
        out_specs=(P(None, "dp", "rep"), P(None, "dp", "rep")),
        check_vma=False,
    )
```

```python
import functools
import math

import jax
import jax.numpy as jnp
import numpy as np
from jax import lax
from jax.experimental import pallas as pl
from jax.experimental.pallas import tpu as pltpu
from jax.sharding import PartitionSpec as P

NX, NY, NZ, NC = 4, 4, 16, 2
STEPS, REQ, TOP_K = 3, 12, 8
D, HEAD_DIM = 4096, 128
EPS = 1e-06
THETA = 1000000.0

LB = 4
PACK = STEPS * LB * REQ
BLOCK = PACK + 16
WIDE = D // NX // LB
STRIDE = 4
CHUNKS = STRIDE
PER = NZ // STRIDE // 2
NEAR = (0, 1, -1, 2)
FIRST, SECOND = 4, 8
SLAB = LB * 2 * STEPS * 2
ROWS = SLAB // LB * NY * NC
CLASSES = 4
SEL = CLASSES * SLAB
HIDE = 128
MESH = pl.DeviceIdType.MESH
F32, BF16 = jnp.float32, jnp.bfloat16


def tables():
    peers, per = NY * NC, SLAB // LB
    out = np.full((peers * SLAB + 8, 128), -1, np.float32)
    row = 0
    for cls in range(CLASSES):
        for lb in range(LB):
            for zz in range(2):
                for s in range(STEPS):
                    for slot in range(2):
                        out[row, 4] = zz * PACK + s * LB * REQ + lb * REQ
                        out[row, 5] = zz * 32 + cls * 8 + s * 2 + slot
                        row += 1
    for lb in range(LB):
        for q in range(peers):
            for r in range(per):
                a, b = (lb * peers + q) * per + r, q * SLAB + lb * per + r
                out[a, 0], out[b, 1] = b, a
    for s in range(STEPS):
        for lb in range(LB):
            for i in range(REQ):
                a, b = (s * LB + lb) * REQ + i, lb * 48 + s * 16 + i
                out[a, 2], out[b, 3] = b, a
    exponent = np.arange(HEAD_DIM // 2, dtype=np.float32) * np.float32(2.0 / HEAD_DIM)
    frequency = np.power(np.float32(THETA), -exponent).astype(np.float32)
    out[peers * SLAB :] = np.concatenate([frequency, frequency])
    return out


def dot(a, b):
    return jnp.dot(a, b, preferred_element_type=F32)


def iota(shape, axis):
    return lax.broadcasted_iota(jnp.int32, shape, axis)


def one_hot(column, width):
    at = iota((column.shape[0], width), 1).astype(F32)
    return jnp.where(at == column, 1.0, 0.0).astype(BF16)


def kernel(
    q_hbm, k_hbm, v_hbm, q_gain_hbm, k_gain_hbm, pool_hbm, table_hbm, len_hbm, out_hbm, slots_hbm,
    hid_hbm, ln_hbm, ids_hbm, logits_hbm, w_gate, w_up, w_down, const_hbm,
    attn, moe,
    q_in, k_in, v_in, q_gain, k_gain, pool, page_table, lengths, out_pages, in_slots,
    hid, ln_gain, ids, logits, const,
    spread, perm, perm_back, pack, unpack_rows, q_rows, k_rows, v_rows, cosines, sines, attn_rows,
    natural, leave, arrive, stat, rows, chosen, taken, w_in, w_out,
    part_own, part_out, part_in, hidden, back_out, back_in, kept, home_out, home_in, last_out, last_in,
    local_sem, load_sem, page_sem, stat_sem, w_sem, row_sem, taken_sem,
    part_sem, hidden_sem, back_sem, home_sem, last_sem,
):
    dp, x = lax.axis_index("dp"), lax.axis_index("rep")
    y, z, c = dp // (NZ * NC), (dp // NC) % NZ, dp % NC
    q = y * NC + c
    mine = z // STRIDE
    across = (((y + 2) % NY * NZ + z) * NC + c, x)

    def along_x(by):
        return (dp, (x + by) % NX)

    def along_z(by):
        return ((y * NZ + (z + by + NZ) % NZ) * NC + c, x)

    def peer(by):
        other = (q + by) % (NY * NC)
        return other, ((other // NC * NZ + z) * NC + other % NC, x)

    def send(src, dst, sem, at, device):
        return pltpu.make_async_remote_copy(
            src_ref=src, dst_ref=dst, send_sem=sem.at[(0,) + at], recv_sem=sem.at[(1,) + at],
            device_id=device, device_id_type=MESH,
        )

    def page_copy():
        return send(leave, arrive, page_sem, (), across)

    def stat_copies():
        return [send(stat.at[0], stat.at[by], stat_sem, (by,), along_x(by)) for by in (1, 2, 3)]

    def weight_copies(by):
        to = (x + by) % NX
        piece = pl.ds(to * (D // NX), D // NX)
        return [
            send(w.at[piece, :], w_in.at[by, :, pl.ds(n * HIDE, HIDE)], w_sem, (by, n), along_x(by))
            for n, w in enumerate((w_gate, w_up))
        ]

    def far_copies():
        return [
            send(rows.at[mine], rows.at[mine], row_sem, (a,), along_z(-STRIDE * a)) for a in (1, 2, 3)
        ]

    def near_copies(n):
        if n < 3:
            pieces = ((pl.ds(0, STRIDE), pl.ds(STRIDE * n, STRIDE), 3 + n, -NEAR[n]),)
        else:
            pieces = ((pl.ds(0, 2), pl.ds(12, 2), 6, -2), (pl.ds(2, 2), pl.ds(14, 2), 7, 2))
        return [send(rows.at[a], rows.at[b], row_sem, (at,), along_z(by)) for a, b, at, by in pieces]

    def taken_copy(ch, by):
        other, device = peer(by)
        cls = other // NC % 2 * NC + other % NC
        return send(chosen.at[ch, cls], taken.at[ch, q], taken_sem, (ch, by), device)

    def part_copy(ch, by):
        return send(part_out.at[ch, by], part_in.at[ch, by], part_sem, (ch, by), along_x(by))

    def hidden_copy(ch, by):
        return send(hidden.at[ch, 0], hidden.at[ch, by], hidden_sem, (ch, by), along_x(by))

    def back_copy(ch, by):
        other, device = peer(by)
        return send(back_out.at[ch, other], back_in.at[ch, q], back_sem, (ch, by), device)

    def home_copies(n):
        if n < 3:
            return [send(home_out.at[n], home_in.at[n], home_sem, (n,), along_z(NEAR[n]))]
        return [
            send(home_out.at[3, at], home_in.at[3, at], home_sem, (3 + m,), along_z(by))
            for m, (at, by) in enumerate(((pl.ds(0, 2), 2), (pl.ds(2, 2), -2)))
        ]

    def last_copy(a):
        return send(last_out.at[a], last_in.at[a], last_sem, (a,), along_z(STRIDE * a))

    loads = {
        name: pltpu.make_async_copy(src, dst, load_sem.at[n])
        for n, (name, src, dst) in enumerate((
            ("hid", hid_hbm, hid), ("out", out_hbm, out_pages), ("pool", pool_hbm, pool),
            ("ln", ln_hbm, ln_gain), ("ids", ids_hbm, ids), ("logits", logits_hbm, logits),
            ("const", const_hbm, const), ("len", len_hbm, lengths), ("table", table_hbm, page_table),
            ("slots", slots_hbm, in_slots), ("k", k_hbm, k_in), ("v", v_hbm, v_in),
            ("k_gain", k_gain_hbm, k_gain), ("q_gain", q_gain_hbm, q_gain), ("q", q_hbm, q_in),
        ))
    }
    for copy in loads.values():
        copy.start()
    own = pl.ds(x * (D // NX), D // NX)
    local = [
        pltpu.make_async_copy(w.at[own, :], w_in.at[0, :, pl.ds(n * HIDE, HIDE)], local_sem.at[n])
        for n, w in enumerate((w_gate, w_up))
    ]
    for by in range(NX):
        src = pl.ds((x + NX - by) % NX * HIDE, HIDE)
        local.append(
            pltpu.make_async_copy(w_down.at[src, :], w_out.at[pl.ds(by * HIDE, HIDE), :], local_sem.at[2 + by])
        )
    barrier = pltpu.get_barrier_semaphore()
    devices = [along_z(by) for by in (1, -1, 2, -2, 4, -4, 8)]
    devices += [along_x(by) for by in (1, 2, 3)] + [peer(by)[1] for by in range(1, 8)]
    for device in devices:
        pl.semaphore_signal(barrier, inc=1, device_id=device, device_id_type=MESH)
    for copy in local:
        copy.start()
    loads["hid"].wait()
    stat[0] = jnp.zeros((STEPS, 16, 128), F32)
    natural[...] = jnp.zeros((STEPS * 16, D // NX), BF16)
    for s in range(STEPS):
        values = hid[s].astype(F32)
        square = jnp.sum(values * values, axis=1, keepdims=True)
        stat[0, s, 0:REQ, :] = jnp.broadcast_to(square, (REQ, 128))
    pl.semaphore_wait(barrier, len(devices))

    for copy in stat_copies():
        copy.start()
    for by in (1, 3, 2):
        for copy in weight_copies(by):
            copy.start()
    loads["out"].wait()
    loads["pool"].wait()
    for n in range(8):
        leave[n] = pool[out_pages[n]]
    page_copy().start()

    for name in ("ln", "ids", "logits", "const"):
        loads[name].wait()
    expert, token = iota((64, REQ), 0), iota((64, REQ), 1).astype(F32)
    lane = iota((64, 128), 1)
    parts = [jnp.zeros((64, 128), F32) for _ in range(3)]
    for s in range(STEPS):
        raw = logits[s]
        expo = jnp.exp(raw - jnp.max(raw, axis=0, keepdims=True))
        share = expo / jnp.sum(expo, axis=0, keepdims=True)
        named = jnp.zeros((64, REQ), F32)
        weight = jnp.zeros((64, REQ), F32)
        for k in range(TOP_K):
            hit = ids[s, k : k + 1, :] == expert
            named = jnp.where(hit, 1.0, named)
            weight = jnp.where(hit, share[k : k + 1, :], weight)
        first = jnp.min(jnp.where(named > 0, token, 512.0), axis=1, keepdims=True)
        second = jnp.max(jnp.where(named > 0, token, -1.0), axis=1, keepdims=True)
        second = jnp.where(second > first, second, 512.0)
        for slot, row in ((0, first), (1, second)):
            given = jnp.sum(jnp.where(token == row, weight, 0.0), axis=1, keepdims=True)
            high = given.astype(BF16).astype(F32)
            for n, column in enumerate((row, high, given - high)):
                parts[n] = jnp.where(lane == 2 * s + slot, column, parts[n])
    turned = jnp.transpose(jnp.concatenate(parts + [jnp.zeros((64, 128), F32)], axis=0))[0:8].astype(BF16)
    place, lane = iota((256, 128), 0), iota((256, 128), 1)
    part = place // 64
    here = (lane // NZ == part) & (part < 3)
    blocks = []
    for cls in range(CLASSES):
        wanted = (cls // NC) * 32 + cls % NC + 2 * (lane % NZ)
        blocks.append(dot(turned, jnp.where(here & (place % 64 == wanted), 1.0, 0.0).astype(BF16)))
    for half in range(2):
        rows[mine, PACK:BLOCK, half * 128 : half * 128 + 128] = jnp.concatenate(
            blocks[2 * half : 2 * half + 2], axis=0
        ).astype(BF16)
    pack[...] = one_hot(const[0:PACK, 2:3], LB * 48)

    for copy in stat_copies():
        copy.wait_recv()
    gain_rows = ln_gain[pl.ds(x * 8, 8), :]
    gain = jnp.concatenate([gain_rows[n : n + 1] for n in range(8)], axis=1)
    for s in range(STEPS):
        mean = (stat[0, s] + stat[1, s] + stat[2, s] + stat[3, s]) * (1.0 / D)
        scale = lax.rsqrt(mean[0:REQ, 0:1] + EPS)
        natural[s * 16 : s * 16 + REQ, :] = (hid[s].astype(F32) * scale * gain).astype(BF16)
    whole = natural[...]
    stack = jnp.concatenate([whole[:, lb * WIDE : (lb + 1) * WIDE] for lb in range(LB)], axis=0)
    rows[mine, 0:PACK, :] = dot(pack[...], stack).astype(BF16)
    for copy in far_copies():
        copy.start()

    spread[...] = one_hot(const[0:SEL, 5:6], 64)
    perm[...] = one_hot(const[0 : NY * NC * SLAB, 0:1], NY * NC * SLAB)
    perm_back[...] = one_hot(const[0 : NY * NC * SLAB, 1:2], NY * NC * SLAB)
    unpack_rows[...] = one_hot(const[0 : LB * 48, 3:4], PACK)
    for name in ("len", "k", "v", "k_gain", "q_gain", "q", "table", "slots"):
        loads[name].wait()

    def normalize(values, gain):
        mean_square = jnp.mean(values * values, axis=-1, keepdims=True)
        return values * lax.rsqrt(mean_square + EPS) * gain

    request = iota((16, 128), 0)
    start = jnp.zeros((16, 128), jnp.int32)
    for i in range(REQ):
        start = jnp.where(request == i, lengths[i], start)
    sign = jnp.where(iota((16, 128), 1) < 64, -1.0, 1.0)
    frequency = const[NY * NC * SLAB : NY * NC * SLAB + 1, :]
    for s in range(STEPS):
        angle = (start + s).astype(F32) * frequency
        cosines[s] = jnp.cos(angle)
        sines[s] = jnp.sin(angle) * sign
        keys = normalize(k_in[s].astype(F32), k_gain[...])
        k_rows[s, 0:REQ, :] = keys * cosines[s, 0:REQ] + pltpu.roll(keys, 64, axis=1) * sines[s, 0:REQ]
        v_rows[s, 0:REQ, :] = v_in[s].astype(F32)
        q_rows[s, 0:REQ, :] = q_in[s].astype(F32)

    def unpack(g):
        pair = rows[pl.ds(2 * g, 2), PACK:BLOCK, :]
        pair = jnp.concatenate([pair[zz, :, h * 128 : h * 128 + 128] for zz in range(2) for h in range(2)], axis=0)
        wide = dot(spread[...], pair)
        lane = iota((SEL, 128), 1)
        code = jnp.sum(jnp.where(lane == z, wide, 0.0), axis=1, keepdims=True) + const[0:SEL, 4:5]
        weight = jnp.sum(
            jnp.where((lane == z + NZ) | (lane == z + 2 * NZ), wide, 0.0), axis=1, keepdims=True
        )
        return code, weight

    def choose(ch):
        for u in range(PER):
            g = ch * PER + u
            code, _ = unpack(g)
            picked = dot(one_hot(code, 2 * PACK), rows[pl.ds(2 * g, 2), 0:PACK, :].reshape(2 * PACK, WIDE)).astype(BF16)
            chosen[ch, :, u * SLAB : (u + 1) * SLAB, :] = picked.reshape(CLASSES, SLAB, WIDE)
        for by in range(1, 8):
            taken_copy(ch, by).start()
        taken[ch, q] = chosen[ch, y % 2 * NC + c]

    scaling = 1.0 / math.sqrt(HEAD_DIM)

    def attend(i, carry):
        pages = []
        for n in range(4):
            at = page_table[n, i]
            moved_to = at
            for m in range(8):
                moved_to = jnp.where(in_slots[m] == at, 48 + m, moved_to)
            pages.append(jnp.where(moved_to < 48, pool[at], arrive[jnp.maximum(moved_to - 48, 0)]))
        row = iota((16, 128), 0)
        extra = jnp.zeros((16, 128), F32)
        asked, cos, sin = [], [], []
        for s in range(STEPS):
            extra = jnp.where(row == 2 * s, k_rows[s, pl.ds(i, 1), :], extra)
            extra = jnp.where(row == 2 * s + 1, v_rows[s, pl.ds(i, 1), :], extra)
            line = q_rows[s, pl.ds(i, 1), :]
            asked += [line[:, h * HEAD_DIM : (h + 1) * HEAD_DIM] for h in range(16)]
            cos.append(jnp.broadcast_to(cosines[s, pl.ds(i, 1), :], (16, 128)))
            sin.append(jnp.broadcast_to(sines[s, pl.ds(i, 1), :], (16, 128)))
        context = jnp.concatenate(pages + [extra.astype(BF16), jnp.zeros((112, 128), BF16)], axis=0)
        asked = normalize(jnp.concatenate(asked, axis=0), q_gain[...])
        asked = asked * jnp.concatenate(cos, axis=0) + pltpu.roll(asked, 64, axis=1) * jnp.concatenate(sin, axis=0)
        scores = lax.dot_general(
            asked.astype(BF16), context, (((1,), (1,)), ((), ())), preferred_element_type=F32
        ) * scaling
        at, step = iota((48, 640), 1), iota((48, 640), 0) // 16
        known = at < 2 * lengths[i]
        added = (at >= 512) & (at <= 512 + 2 * step)
        valid = (known | added) & (at % 2 == 0)
        scores = jnp.where(valid, scores, -1e30)
        top = jnp.max(scores, axis=-1, keepdims=True)
        expos = jnp.where(valid, jnp.exp(scores - top), 0.0)
        probs = expos / jnp.sum(expos, axis=-1, keepdims=True)
        probs = pltpu.roll(probs, 1, axis=1).astype(BF16)
        mixed = dot(probs, context)
        for s in range(STEPS):
            attn_rows[s, pl.ds(i, 1), :] = jnp.concatenate(
                [mixed[s * 16 + h : s * 16 + h + 1] for h in range(16)], axis=1
            )
        return carry

    for copy in far_copies():
        copy.wait_recv()
    for n in (1, 2, 3):
        for copy in near_copies(n):
            copy.start()
    choose(0)
    page_copy().wait_recv()
    lax.fori_loop(0, FIRST, attend, 0)

    def choose_next(ch, carry):
        for n in (1, 2, 3):
            @pl.when(jnp.int32(ch) == n)
            def _(n=n):
                for copy in near_copies(n):
                    copy.wait_recv()

        choose(ch)
        return carry

    lax.fori_loop(1, CHUNKS - 1, choose_next, 0)

    for copy in local:
        copy.wait()
    for by in (1, 2, 3):
        for copy in weight_copies(by):
            copy.wait_recv()

    def first_matmul(ch):
        for by in range(1, 8):
            taken_copy(ch, by).wait_recv()
        pieces = []
        for u in range(PER):
            slabs = taken[ch, :, u * SLAB : (u + 1) * SLAB, :].reshape(NY * NC * SLAB, WIDE)
            block = dot(perm[...], slabs).astype(BF16)
            pieces.append(
                jnp.concatenate([block[lb * ROWS : (lb + 1) * ROWS] for lb in range(LB)], axis=1)
            )
        inputs = jnp.concatenate(pieces, axis=0)
        for by in (2, 1, 3):
            part_out[ch, by] = dot(inputs, w_in[(NX - by) % NX]).astype(BF16)
            part_copy(ch, by).start()
        part_own[ch] = dot(inputs, w_in[0])

    def activate(ch):
        for by in (1, 2, 3):
            part_copy(ch, by).wait_recv()
        both = part_own[ch] + part_in[ch, 1].astype(F32) + part_in[ch, 2].astype(F32) + part_in[ch, 3].astype(F32)
        gate, upper = both[:, :HIDE], both[:, HIDE:]
        hidden[ch, 0] = (gate / (1.0 + jnp.exp(-gate)) * upper).astype(BF16)
        for by in (2, 1, 3):
            hidden_copy(ch, by).start()

    def second_matmul(ch):
        for by in (1, 2, 3):
            hidden_copy(ch, by).wait_recv()
        units = jnp.concatenate([hidden[ch, by] for by in range(NX)], axis=1)
        made = dot(units, w_out[...]).astype(BF16)
        for u in range(PER):
            part = made[u * ROWS : (u + 1) * ROWS]
            stack = jnp.concatenate([part[:, lb * WIDE : (lb + 1) * WIDE] for lb in range(LB)], axis=0)
            slabs = dot(perm_back[...], stack).astype(BF16)
            back_out[ch, :, u * SLAB : (u + 1) * SLAB, :] = slabs.reshape(NY * NC, SLAB, WIDE)
        for by in range(1, 8):
            back_copy(ch, by).start()
        back_in[ch, q] = back_out[ch, q]

    def combine(ch):
        for by in range(1, 8):
            back_copy(ch, by).wait_recv()
        for u in range(PER):
            g = ch * PER + u
            code, weight = unpack(g)
            slabs = back_in[ch, :, u * SLAB : (u + 1) * SLAB, :].astype(F32)
            both = (slabs[:CLASSES] + slabs[CLASSES:]).reshape(SEL, WIDE)
            both = (both * weight).astype(BF16)
            diagonal = iota((SEL, SEL), 0) == iota((SEL, SEL), 1)
            code_row = jnp.sum(jnp.where(diagonal, code, 0.0), axis=0, keepdims=True)
            at = iota((2 * PACK, SEL), 0).astype(F32)
            sums = dot(jnp.where(at == code_row, 1.0, 0.0).astype(BF16), both)
            home_out[ch, 2 * u : 2 * u + 2] = sums.astype(BF16).reshape(2, PACK, WIDE)

            @pl.when(ch == 0)
            def _(u=u, sums=sums):
                kept[2 * u : 2 * u + 2] = sums.reshape(2, PACK, WIDE)

        for n in (1, 2, 3):
            @pl.when(ch == n)
            def _(n=n):
                for copy in home_copies(n):
                    copy.start()

    def experts(it, carry):
        @pl.when(it == 1)
        def _():
            choose_next(CHUNKS - 1, 0)

        @pl.when(it < CHUNKS)
        def _():
            first_matmul((it + 1) % CHUNKS)

        @pl.when((it >= 1) & (it < CHUNKS + 1))
        def _():
            activate(it % CHUNKS)

        @pl.when((it >= 2) & (it < CHUNKS + 2))
        def _():
            second_matmul((it - 1) % CHUNKS)

        @pl.when(it >= 3)
        def _():
            combine((it - 2) % CHUNKS)

        return carry

    lax.fori_loop(0, CHUNKS + 3, experts, 0)

    lax.fori_loop(FIRST, SECOND, attend, 0)
    for n in (1, 2, 3):
        for copy in home_copies(n):
            copy.wait_recv()

    def gathered(a):
        at = (mine + a) % STRIDE
        summed = kept[at]
        for n in (1, 2, 3):
            summed = summed + home_in[n, at].astype(F32)
        return summed

    for a in (2, 1, 3):
        last_out[a] = gathered(a).astype(BF16)
        last_copy(a).start()
    lax.fori_loop(SECOND, REQ, attend, 0)
    for s in range(STEPS):
        attn[s] = attn_rows[s, 0:REQ, :].astype(BF16)
    for a in (1, 2, 3):
        last_copy(a).wait_recv()
    summed = gathered(0)
    for a in (1, 2, 3):
        summed = summed + last_in[a].astype(F32)
    flat = dot(unpack_rows[...], summed.astype(BF16)).astype(BF16)
    for s in range(STEPS):
        moe[s] = jnp.concatenate(
            [flat[lb * 48 + s * 16 : lb * 48 + s * 16 + 16] for lb in range(LB)], axis=1
        )[0:REQ]

    page_copy().wait_send()
    for copy in stat_copies() + far_copies():
        copy.wait_send()
    for n in (1, 2, 3):
        for copy in weight_copies(n) + near_copies(n) + home_copies(n) + [last_copy(n)]:
            copy.wait_send()

    def drain(ch, carry):
        for by in (1, 2, 3):
            part_copy(ch, by).wait_send()
            hidden_copy(ch, by).wait_send()
        for by in range(1, 8):
            taken_copy(ch, by).wait_send()
            back_copy(ch, by).wait_send()
        return carry

    lax.fori_loop(0, CHUNKS, drain, 0)


def local(
    q_raw, k_raw, v_raw, q_gain, k_gain, kv_pool, page_table, cache_len, out_pages, in_slots,
    hidden_in, ln_gain, route_ids, route_logits, w_gate, w_up, w_down,
):
    hbm = pl.BlockSpec(memory_space=pltpu.HBM)
    vmem = pl.BlockSpec(memory_space=pltpu.VMEM)
    peers, part = NY * NC, D // NX
    sem, buf = pltpu.SemaphoreType.DMA, pltpu.VMEM
    const = tables()
    operands = (
        q_raw, k_raw, v_raw, q_gain.reshape(1, HEAD_DIM), k_gain.reshape(1, HEAD_DIM),
        kv_pool.reshape(48, 128, HEAD_DIM), page_table.T, cache_len, out_pages, in_slots,
        hidden_in, ln_gain.reshape(D // 128, 128), route_ids.transpose(0, 2, 1), route_logits.transpose(0, 2, 1),
        w_gate.reshape(D, HIDE), w_up.reshape(D, HIDE), w_down.reshape(NX * HIDE, part), jnp.asarray(const),
    )
    held = [
        pltpu.SMEM(a.shape, a.dtype) if n in (6, 7, 8, 9) else buf(a.shape, a.dtype)
        for n, a in enumerate(operands)
        if n not in (14, 15, 16)
    ]
    attn, moe = pl.pallas_call(
        kernel,
        out_shape=(
            jax.ShapeDtypeStruct((STEPS, REQ, 16 * HEAD_DIM), BF16),
            jax.ShapeDtypeStruct((STEPS, REQ, part), BF16),
        ),
        in_specs=[hbm] * len(operands),
        out_specs=(vmem, vmem),
        scratch_shapes=held + [
            buf((SEL, 64), BF16),
            buf((peers * SLAB, peers * SLAB), BF16),
            buf((peers * SLAB, peers * SLAB), BF16),
            buf((PACK, LB * 48), BF16),
            buf((LB * 48, PACK), BF16),
            buf((STEPS, 16, 16 * HEAD_DIM), F32),
            buf((STEPS, 16, HEAD_DIM), F32),
            buf((STEPS, 16, HEAD_DIM), F32),
            buf((STEPS, 16, HEAD_DIM), F32),
            buf((STEPS, 16, HEAD_DIM), F32),
            buf((STEPS, 16, 16 * HEAD_DIM), F32),
            buf((STEPS * 16, part), BF16),
            buf((8, 128, HEAD_DIM), BF16),
            buf((8, 128, HEAD_DIM), BF16),
            buf((NX, STEPS, 16, 128), F32),
            buf((NZ, BLOCK, WIDE), BF16),
            buf((CHUNKS, CLASSES, PER * SLAB, WIDE), BF16),
            buf((CHUNKS, peers, PER * SLAB, WIDE), BF16),
            buf((NX, part, 2 * HIDE), BF16),
            buf((NX * HIDE, part), BF16),
            buf((CHUNKS, PER * ROWS, 2 * HIDE), F32),
            buf((CHUNKS, NX, PER * ROWS, 2 * HIDE), BF16),
            buf((CHUNKS, NX, PER * ROWS, 2 * HIDE), BF16),
            buf((CHUNKS, NX, PER * ROWS, HIDE), BF16),
            buf((CHUNKS, peers, PER * SLAB, WIDE), BF16),
            buf((CHUNKS, peers, PER * SLAB, WIDE), BF16),
            buf((STRIDE, PACK, WIDE), F32),
            buf((CHUNKS, STRIDE, PACK, WIDE), BF16),
            buf((CHUNKS, STRIDE, PACK, WIDE), BF16),
            buf((STRIDE, PACK, WIDE), BF16),
            buf((STRIDE, PACK, WIDE), BF16),
            sem((6,)),
            sem((15,)),
            sem((2,)),
            sem((2, NX)),
            sem((2, NX, 2)),
            sem((2, 8)),
            sem((2, CHUNKS, peers)),
            sem((2, CHUNKS, NX)),
            sem((2, CHUNKS, NX)),
            sem((2, CHUNKS, peers)),
            sem((2, 5)),
            sem((2, STRIDE)),
        ],
        compiler_params=pltpu.CompilerParams(
            collective_id=0, has_side_effects=True, vmem_limit_bytes=63 * 1024 * 1024
        ),
    )(*operands)
    return attn, moe


def solution(mesh):
    return jax.shard_map(
        local,
        mesh=mesh,
        in_specs=(
            P(None, "dp", "rep"),
            P(None, "dp", "rep"),
            P(None, "dp", "rep"),
            P(),
            P(),
            P("dp", None, None, "rep"),
            P("dp", None),
            P("dp"),
            P("dp"),
            P("dp"),
            P(None, "dp", "rep"),
            P(),
            P(None, "dp", None),
            P(None, "dp", None),
            P("dp", None, "rep"),
            P("dp", None, "rep"),
            P("dp", None, "rep"),
        ),
        out_specs=(P(None, "dp", "rep"), P(None, "dp", "rep")),
        check_vma=False,
    )
```

```python
import functools
import math

import jax
import jax.numpy as jnp
import numpy as np
from jax import lax
from jax.experimental import pallas as pl
from jax.experimental.pallas import tpu as pltpu
from jax.sharding import PartitionSpec as P

NX, NY, NZ, NC = 4, 4, 16, 2
STEPS, REQ, TOP_K = 3, 12, 8
D, HEAD_DIM = 4096, 128
EPS = 1e-06
THETA = 1000000.0

LB = 4
PACK = STEPS * LB * REQ
BLOCK = PACK + 16
WIDE = D // NX // LB
STRIDE = 4
CHUNKS = STRIDE
PER = NZ // STRIDE
NEAR = (0, 1, -1, 2)
FIRST, SECOND = 4, 8
PART = PER * STEPS * 2
SLAB = LB * PART
ROWS = PART * NY * NC
CLASSES = 4
SEL = CLASSES * SLAB
HIDE = 128
MESH = pl.DeviceIdType.MESH
F32, BF16 = jnp.float32, jnp.bfloat16


def tables():
    out = np.full((SEL + 8, 128), -1, np.float32)
    row = 0
    for cls in range(CLASSES):
        for lb in range(LB):
            for j in range(PER):
                for s in range(STEPS):
                    for slot in range(2):
                        out[row, 0] = j * PACK + s * LB * REQ + lb * REQ
                        out[row, 1] = j * 32 + cls * 8 + s * 2 + slot
                        row += 1
    for s in range(STEPS):
        for lb in range(LB):
            for i in range(REQ):
                a, b = (s * LB + lb) * REQ + i, lb * 48 + s * 16 + i
                out[a, 2], out[b, 3] = b, a
    exponent = np.arange(HEAD_DIM // 2, dtype=np.float32) * np.float32(2.0 / HEAD_DIM)
    frequency = np.power(np.float32(THETA), -exponent).astype(np.float32)
    out[SEL:] = np.concatenate([frequency, frequency])
    return out


def dot(a, b):
    return jnp.dot(a, b, preferred_element_type=F32)


def iota(shape, axis):
    return lax.broadcasted_iota(jnp.int32, shape, axis)


def one_hot(column, width):
    at = iota((column.shape[0], width), 1).astype(F32)
    return jnp.where(at == column, 1.0, 0.0).astype(BF16)


def kernel(
    q_hbm, k_hbm, v_hbm, q_gain_hbm, k_gain_hbm, pool_hbm, table_hbm, len_hbm, out_hbm, slots_hbm,
    hid_hbm, ln_hbm, ids_hbm, logits_hbm, w_gate, w_up, w_down, const_hbm,
    attn, moe,
    q_in, k_in, v_in, q_gain, k_gain, pool, page_table, lengths, out_pages, in_slots,
    hid, ln_gain, ids, logits, const,
    spread, code_rows, shares, pack, unpack_rows, q_rows, k_rows, v_rows, cosines, sines, attn_rows,
    natural, leave, arrive, stat, rows, near_out, chosen, taken, w_in, w_out,
    part_own, part_out, part_in, hidden, back_out, back_in, kept, home_out, home_in, last_out, last_in,
    local_sem, load_sem, page_sem, stat_sem, w_sem, row_sem, taken_sem,
    part_sem, hidden_sem, back_sem, home_sem, last_sem,
):
    dp, x = lax.axis_index("dp"), lax.axis_index("rep")
    y, z, c = dp // (NZ * NC), (dp // NC) % NZ, dp % NC
    q = y * NC + c
    mine = z // STRIDE
    across = (((y + 2) % NY * NZ + z) * NC + c, x)

    def along_x(by):
        return (dp, (x + by) % NX)

    def along_z(by):
        return ((y * NZ + (z + by + NZ) % NZ) * NC + c, x)

    def peer(by):
        other = (q + by) % (NY * NC)
        return other, ((other // NC * NZ + z) * NC + other % NC, x)

    def send(src, dst, sem, at, device):
        return pltpu.make_async_remote_copy(
            src_ref=src, dst_ref=dst, send_sem=sem.at[(0,) + at], recv_sem=sem.at[(1,) + at],
            device_id=device, device_id_type=MESH,
        )

    def page_copy():
        return send(leave, arrive, page_sem, (), across)

    def stat_copies():
        return [send(stat.at[0], stat.at[by], stat_sem, (by,), along_x(by)) for by in (1, 2, 3)]

    def weight_copies(by):
        to = (x + by) % NX
        piece = pl.ds(to * (D // NX), D // NX)
        return [
            send(w.at[piece, :], w_in.at[by, :, pl.ds(n * HIDE, HIDE)], w_sem, (by, n), along_x(by))
            for n, w in enumerate((w_gate, w_up))
        ]

    def far_copies():
        return [
            send(rows.at[mine], rows.at[mine], row_sem, (a,), along_z(-STRIDE * a)) for a in (1, 2, 3)
        ]

    def near_copies(n):
        if n < 3:
            return [send(near_out.at[n], chosen.at[n], row_sem, (3 + n,), along_z(-NEAR[n]))]
        return [
            send(near_out.at[3, at], chosen.at[3, at], row_sem, (6 + m,), along_z(by))
            for m, (at, by) in enumerate(((pl.ds(0, 2), -2), (pl.ds(2, 2), 2)))
        ]

    def taken_copy(ch, by):
        other, device = peer(by)
        cls = other // NC % 2 * NC + other % NC
        return send(chosen.at[ch, cls], taken.at[ch, q], taken_sem, (ch, by), device)

    def part_copy(ch, by):
        return send(part_out.at[ch, by], part_in.at[ch, by], part_sem, (ch, by), along_x(by))

    def hidden_copy(ch, by):
        return send(hidden.at[ch, 0], hidden.at[ch, by], hidden_sem, (ch, by), along_x(by))

    def back_copy(ch, by):
        other, device = peer(by)
        return send(back_out.at[ch, other], back_in.at[ch, q], back_sem, (ch, by), device)

    def home_copies(n):
        if n < 3:
            return [send(home_out.at[n], home_in.at[n], home_sem, (n,), along_z(NEAR[n]))]
        return [
            send(home_out.at[3, at], home_in.at[3, at], home_sem, (3 + m,), along_z(by))
            for m, (at, by) in enumerate(((pl.ds(0, 2), 2), (pl.ds(2, 2), -2)))
        ]

    def last_copy(a):
        return send(last_out.at[a], last_in.at[a], last_sem, (a,), along_z(STRIDE * a))

    loads = {
        name: pltpu.make_async_copy(src, dst, load_sem.at[n])
        for n, (name, src, dst) in enumerate((
            ("hid", hid_hbm, hid), ("out", out_hbm, out_pages), ("pool", pool_hbm, pool),
            ("ln", ln_hbm, ln_gain), ("ids", ids_hbm, ids), ("logits", logits_hbm, logits),
            ("const", const_hbm, const), ("len", len_hbm, lengths), ("table", table_hbm, page_table),
            ("slots", slots_hbm, in_slots), ("k", k_hbm, k_in), ("v", v_hbm, v_in),
            ("k_gain", k_gain_hbm, k_gain), ("q_gain", q_gain_hbm, q_gain), ("q", q_hbm, q_in),
        ))
    }
    for copy in loads.values():
        copy.start()
    own = pl.ds(x * (D // NX), D // NX)
    local = [
        pltpu.make_async_copy(w.at[own, :], w_in.at[0, :, pl.ds(n * HIDE, HIDE)], local_sem.at[n])
        for n, w in enumerate((w_gate, w_up))
    ]
    for by in range(NX):
        src = pl.ds((x + NX - by) % NX * HIDE, HIDE)
        local.append(
            pltpu.make_async_copy(w_down.at[src, :], w_out.at[pl.ds(by * HIDE, HIDE), :], local_sem.at[2 + by])
        )
    barrier = pltpu.get_barrier_semaphore()
    devices = [along_z(by) for by in (1, -1, 2, -2, 4, -4, 8)]
    devices += [along_x(by) for by in (1, 2, 3)] + [peer(by)[1] for by in range(1, 8)]
    for device in devices:
        pl.semaphore_signal(barrier, inc=1, device_id=device, device_id_type=MESH)
    for copy in local:
        copy.start()
    loads["hid"].wait()
    stat[0] = jnp.zeros((STEPS, 16, 128), F32)
    natural[...] = jnp.zeros((STEPS * 16, D // NX), BF16)
    for s in range(STEPS):
        values = hid[s].astype(F32)
        square = jnp.sum(values * values, axis=1, keepdims=True)
        stat[0, s, 0:REQ, :] = jnp.broadcast_to(square, (REQ, 128))
    pl.semaphore_wait(barrier, len(devices))

    for copy in stat_copies():
        copy.start()
    for by in (1, 3, 2):
        for copy in weight_copies(by):
            copy.start()
    loads["out"].wait()
    loads["pool"].wait()
    for n in range(8):
        leave[n] = pool[out_pages[n]]
    page_copy().start()

    for name in ("ln", "ids", "logits", "const"):
        loads[name].wait()
    expert, token = iota((64, REQ), 0), iota((64, REQ), 1).astype(F32)
    lane = iota((64, 128), 1)
    parts = [jnp.zeros((64, 128), F32) for _ in range(3)]
    for s in range(STEPS):
        raw = logits[s]
        expo = jnp.exp(raw - jnp.max(raw, axis=0, keepdims=True))
        share = expo / jnp.sum(expo, axis=0, keepdims=True)
        named = jnp.zeros((64, REQ), F32)
        weight = jnp.zeros((64, REQ), F32)
        for k in range(TOP_K):
            hit = ids[s, k : k + 1, :] == expert
            named = jnp.where(hit, 1.0, named)
            weight = jnp.where(hit, share[k : k + 1, :], weight)
        first = jnp.min(jnp.where(named > 0, token, 512.0), axis=1, keepdims=True)
        second = jnp.max(jnp.where(named > 0, token, -1.0), axis=1, keepdims=True)
        second = jnp.where(second > first, second, 512.0)
        for slot, row in ((0, first), (1, second)):
            given = jnp.sum(jnp.where(token == row, weight, 0.0), axis=1, keepdims=True)
            high = given.astype(BF16).astype(F32)
            for n, column in enumerate((row, high, given - high)):
                parts[n] = jnp.where(lane == 2 * s + slot, column, parts[n])
    turned = jnp.transpose(jnp.concatenate(parts + [jnp.zeros((64, 128), F32)], axis=0))[0:8].astype(BF16)
    place, lane = iota((256, 128), 0), iota((256, 128), 1)
    part = place // 64
    here = (lane // NZ == part) & (part < 3)
    blocks = []
    for cls in range(CLASSES):
        wanted = (cls // NC) * 32 + cls % NC + 2 * (lane % NZ)
        blocks.append(dot(turned, jnp.where(here & (place % 64 == wanted), 1.0, 0.0).astype(BF16)))
    for half in range(2):
        rows[mine, PACK:BLOCK, half * 128 : half * 128 + 128] = jnp.concatenate(
            blocks[2 * half : 2 * half + 2], axis=0
        ).astype(BF16)
    pack[...] = one_hot(const[0:PACK, 2:3], LB * 48)

    for copy in stat_copies():
        copy.wait_recv()
    gain_rows = ln_gain[pl.ds(x * 8, 8), :]
    gain = jnp.concatenate([gain_rows[n : n + 1] for n in range(8)], axis=1)
    for s in range(STEPS):
        mean = (stat[0, s] + stat[1, s] + stat[2, s] + stat[3, s]) * (1.0 / D)
        scale = lax.rsqrt(mean[0:REQ, 0:1] + EPS)
        natural[s * 16 : s * 16 + REQ, :] = (hid[s].astype(F32) * scale * gain).astype(BF16)
    whole = natural[...]
    stack = jnp.concatenate([whole[:, lb * WIDE : (lb + 1) * WIDE] for lb in range(LB)], axis=0)
    rows[mine, 0:PACK, :] = dot(pack[...], stack).astype(BF16)
    for copy in far_copies():
        copy.start()

    spread[...] = one_hot(const[0:SEL, 1:2], PER * 32)
    unpack_rows[...] = one_hot(const[0 : LB * 48, 3:4], PACK)
    for name in ("len", "k", "v", "k_gain", "q_gain", "q", "table", "slots"):
        loads[name].wait()

    def normalize(values, gain):
        mean_square = jnp.mean(values * values, axis=-1, keepdims=True)
        return values * lax.rsqrt(mean_square + EPS) * gain

    request = iota((16, 128), 0)
    start = jnp.zeros((16, 128), jnp.int32)
    for i in range(REQ):
        start = jnp.where(request == i, lengths[i], start)
    sign = jnp.where(iota((16, 128), 1) < 64, -1.0, 1.0)
    frequency = const[SEL : SEL + 1, :]
    for s in range(STEPS):
        angle = (start + s).astype(F32) * frequency
        cosines[s] = jnp.cos(angle)
        sines[s] = jnp.sin(angle) * sign
        keys = normalize(k_in[s].astype(F32), k_gain[...])
        k_rows[s, 0:REQ, :] = keys * cosines[s, 0:REQ] + pltpu.roll(keys, 64, axis=1) * sines[s, 0:REQ]
        v_rows[s, 0:REQ, :] = v_in[s].astype(F32)
        q_rows[s, 0:REQ, :] = q_in[s].astype(F32)

    def choose(n):
        pair = rows[:, PACK:BLOCK, :]
        pair = jnp.concatenate([pair[j, :, h * 128 : h * 128 + 128] for j in range(PER) for h in range(2)], axis=0)
        wide = dot(spread[...], pair)
        lane = iota((SEL, 128), 1)
        if n < 3:
            there = (z + NZ - NEAR[n]) % NZ
        else:
            there = jnp.where(iota((SEL, 128), 0) < SEL // 2, (z + NZ - 2) % NZ, (z + 2) % NZ)
        code = jnp.sum(jnp.where(lane == there, wide, 0.0), axis=1, keepdims=True) + const[0:SEL, 0:1]
        weight = jnp.sum(
            jnp.where((lane == there + NZ) | (lane == there + 2 * NZ), wide, 0.0), axis=1, keepdims=True
        )
        tokens = rows[:, 0:PACK, :].reshape(PER * PACK, WIDE)
        picked = dot(one_hot(code, PER * PACK), tokens).astype(BF16).reshape(CLASSES, SLAB, WIDE)
        if n:
            near_out[n] = picked
            for copy in near_copies(n):
                copy.start()
        else:
            chosen[0] = picked
            forward(0)
        diagonal = iota((SEL, SEL), 0) == iota((SEL, SEL), 1)
        code_row = jnp.sum(jnp.where(diagonal, code, 0.0), axis=0, keepdims=True)
        code_rows[n] = jnp.broadcast_to(code_row, (8, SEL))
        shares[n] = jnp.broadcast_to(weight, (SEL, 128))

    def forward(ch):
        for by in range(1, 8):
            taken_copy(ch, by).start()
        taken[ch, q] = chosen[ch, y % 2 * NC + c]

    scaling = 1.0 / math.sqrt(HEAD_DIM)

    def attend(i, carry):
        pages = []
        for n in range(4):
            at = page_table[n, i]
            moved_to = at
            for m in range(8):
                moved_to = jnp.where(in_slots[m] == at, 48 + m, moved_to)
            pages.append(jnp.where(moved_to < 48, pool[at], arrive[jnp.maximum(moved_to - 48, 0)]))
        row = iota((16, 128), 0)
        extra = jnp.zeros((16, 128), F32)
        asked, cos, sin = [], [], []
        for s in range(STEPS):
            extra = jnp.where(row == 2 * s, k_rows[s, pl.ds(i, 1), :], extra)
            extra = jnp.where(row == 2 * s + 1, v_rows[s, pl.ds(i, 1), :], extra)
            line = q_rows[s, pl.ds(i, 1), :]
            asked += [line[:, h * HEAD_DIM : (h + 1) * HEAD_DIM] for h in range(16)]
            cos.append(jnp.broadcast_to(cosines[s, pl.ds(i, 1), :], (16, 128)))
            sin.append(jnp.broadcast_to(sines[s, pl.ds(i, 1), :], (16, 128)))
        context = jnp.concatenate(pages + [extra.astype(BF16), jnp.zeros((112, 128), BF16)], axis=0)
        asked = normalize(jnp.concatenate(asked, axis=0), q_gain[...])
        asked = asked * jnp.concatenate(cos, axis=0) + pltpu.roll(asked, 64, axis=1) * jnp.concatenate(sin, axis=0)
        scores = lax.dot_general(
            asked.astype(BF16), context, (((1,), (1,)), ((), ())), preferred_element_type=F32
        ) * scaling
        at, step = iota((48, 640), 1), iota((48, 640), 0) // 16
        known = at < 2 * lengths[i]
        added = (at >= 512) & (at <= 512 + 2 * step)
        valid = (known | added) & (at % 2 == 0)
        scores = jnp.where(valid, scores, -1e30)
        top = jnp.max(scores, axis=-1, keepdims=True)
        expos = jnp.where(valid, jnp.exp(scores - top), 0.0)
        probs = expos / jnp.sum(expos, axis=-1, keepdims=True)
        probs = pltpu.roll(probs, 1, axis=1).astype(BF16)
        mixed = dot(probs, context)
        for s in range(STEPS):
            attn_rows[s, pl.ds(i, 1), :] = jnp.concatenate(
                [mixed[s * 16 + h : s * 16 + h + 1] for h in range(16)], axis=1
            )
        return carry

    for copy in far_copies():
        copy.wait_recv()
    for n in (1, 2, 3, 0):
        choose(n)
    page_copy().wait_recv()
    lax.fori_loop(0, FIRST, attend, 0)

    def choose_next(ch, carry):
        for n in (1, 2, 3):
            @pl.when(jnp.int32(ch) == n)
            def _(n=n):
                for copy in near_copies(n):
                    copy.wait_recv()

        forward(ch)
        return carry

    lax.fori_loop(1, CHUNKS - 1, choose_next, 0)

    for copy in local:
        copy.wait()
    for by in (1, 2, 3):
        for copy in weight_copies(by):
            copy.wait_recv()

    def first_matmul(ch):
        for by in range(1, 8):
            taken_copy(ch, by).wait_recv()
        slabs = taken[ch].astype(F32)
        inputs = jnp.concatenate(
            [slabs[:, lb * PART : (lb + 1) * PART, :].reshape(ROWS, WIDE) for lb in range(LB)], axis=1
        ).astype(BF16)
        for by in (2, 1, 3):
            part_out[ch, by] = dot(inputs, w_in[(NX - by) % NX]).astype(BF16)
            part_copy(ch, by).start()
        part_own[ch] = dot(inputs, w_in[0])

    def activate(ch):
        for by in (1, 2, 3):
            part_copy(ch, by).wait_recv()
        both = part_own[ch] + part_in[ch, 1].astype(F32) + part_in[ch, 2].astype(F32) + part_in[ch, 3].astype(F32)
        gate, upper = both[:, :HIDE], both[:, HIDE:]
        hidden[ch, 0] = (gate / (1.0 + jnp.exp(-gate)) * upper).astype(BF16)
        for by in (2, 1, 3):
            hidden_copy(ch, by).start()

    def second_matmul(ch):
        for by in (1, 2, 3):
            hidden_copy(ch, by).wait_recv()
        units = jnp.concatenate([hidden[ch, by] for by in range(NX)], axis=1)
        made = dot(units, w_out[...]).reshape(NY * NC, PART, D // NX)
        back_out[ch] = jnp.concatenate(
            [made[:, :, lb * WIDE : (lb + 1) * WIDE] for lb in range(LB)], axis=1
        ).astype(BF16)
        for by in range(1, 8):
            back_copy(ch, by).start()
        back_in[ch, q] = back_out[ch, q]

    def combine(ch):
        for by in range(1, 8):
            back_copy(ch, by).wait_recv()
        slabs = back_in[ch].astype(F32)
        home_out[ch] = (slabs[:CLASSES] + slabs[CLASSES:]).astype(BF16)

        @pl.when(ch == 0)
        def _():
            home_in[0] = home_out[0]

        for n in (1, 2, 3):
            @pl.when(ch == n)
            def _(n=n):
                for copy in home_copies(n):
                    copy.start()

    def experts(it, carry):
        @pl.when(it == 1)
        def _():
            choose_next(CHUNKS - 1, 0)

        @pl.when(it < CHUNKS)
        def _():
            first_matmul((it + 1) % CHUNKS)

        @pl.when((it >= 1) & (it < CHUNKS + 1))
        def _():
            activate(it % CHUNKS)

        @pl.when((it >= 2) & (it < CHUNKS + 2))
        def _():
            second_matmul((it - 1) % CHUNKS)

        @pl.when(it >= 3)
        def _():
            combine((it - 2) % CHUNKS)

        return carry

    lax.fori_loop(0, CHUNKS + 3, experts, 0)

    lax.fori_loop(FIRST, SECOND, attend, 0)
    for n in (1, 2, 3, 0):
        if n:
            for copy in home_copies(n):
                copy.wait_recv()
        both = (home_in[n].astype(F32).reshape(SEL, WIDE) * shares[n, :, 0:1]).astype(BF16)
        at = iota((PER * PACK, SEL), 0).astype(F32)
        sums = dot(jnp.where(at == code_rows[n, 0:1, :], 1.0, 0.0).astype(BF16), both).reshape(PER, PACK, WIDE)
        kept[...] = sums if n == 1 else kept[...] + sums

    def gathered(a):
        return kept[(mine + a) % STRIDE]

    for a in (2, 1, 3):
        last_out[a] = gathered(a).astype(BF16)
        last_copy(a).start()
    lax.fori_loop(SECOND, REQ, attend, 0)
    for s in range(STEPS):
        attn[s] = attn_rows[s, 0:REQ, :].astype(BF16)
    for a in (1, 2, 3):
        last_copy(a).wait_recv()
    summed = gathered(0)
    for a in (1, 2, 3):
        summed = summed + last_in[a].astype(F32)
    flat = dot(unpack_rows[...], summed.astype(BF16)).astype(BF16)
    for s in range(STEPS):
        moe[s] = jnp.concatenate(
            [flat[lb * 48 + s * 16 : lb * 48 + s * 16 + 16] for lb in range(LB)], axis=1
        )[0:REQ]

    page_copy().wait_send()
    for copy in stat_copies() + far_copies():
        copy.wait_send()
    for n in (1, 2, 3):
        for copy in weight_copies(n) + near_copies(n) + home_copies(n) + [last_copy(n)]:
            copy.wait_send()

    def drain(ch, carry):
        for by in (1, 2, 3):
            part_copy(ch, by).wait_send()
            hidden_copy(ch, by).wait_send()
        for by in range(1, 8):
            taken_copy(ch, by).wait_send()
            back_copy(ch, by).wait_send()
        return carry

    lax.fori_loop(0, CHUNKS, drain, 0)


def local(
    q_raw, k_raw, v_raw, q_gain, k_gain, kv_pool, page_table, cache_len, out_pages, in_slots,
    hidden_in, ln_gain, route_ids, route_logits, w_gate, w_up, w_down,
):
    hbm = pl.BlockSpec(memory_space=pltpu.HBM)
    vmem = pl.BlockSpec(memory_space=pltpu.VMEM)
    peers, part = NY * NC, D // NX
    sem, buf = pltpu.SemaphoreType.DMA, pltpu.VMEM
    const = tables()
    operands = (
        q_raw, k_raw, v_raw, q_gain.reshape(1, HEAD_DIM), k_gain.reshape(1, HEAD_DIM),
        kv_pool.reshape(48, 128, HEAD_DIM), page_table.T, cache_len, out_pages, in_slots,
        hidden_in, ln_gain.reshape(D // 128, 128), route_ids.transpose(0, 2, 1), route_logits.transpose(0, 2, 1),
        w_gate.reshape(D, HIDE), w_up.reshape(D, HIDE), w_down.reshape(NX * HIDE, part), jnp.asarray(const),
    )
    held = [
        pltpu.SMEM(a.shape, a.dtype) if n in (6, 7, 8, 9) else buf(a.shape, a.dtype)
        for n, a in enumerate(operands)
        if n not in (14, 15, 16)
    ]
    attn, moe = pl.pallas_call(
        kernel,
        out_shape=(
            jax.ShapeDtypeStruct((STEPS, REQ, 16 * HEAD_DIM), BF16),
            jax.ShapeDtypeStruct((STEPS, REQ, part), BF16),
        ),
        in_specs=[hbm] * len(operands),
        out_specs=(vmem, vmem),
        scratch_shapes=held + [
            buf((SEL, PER * 32), BF16),
            buf((CHUNKS, 8, SEL), F32),
            buf((CHUNKS, SEL, 128), F32),
            buf((PACK, LB * 48), BF16),
            buf((LB * 48, PACK), BF16),
            buf((STEPS, 16, 16 * HEAD_DIM), F32),
            buf((STEPS, 16, HEAD_DIM), F32),
            buf((STEPS, 16, HEAD_DIM), F32),
            buf((STEPS, 16, HEAD_DIM), F32),
            buf((STEPS, 16, HEAD_DIM), F32),
            buf((STEPS, 16, 16 * HEAD_DIM), F32),
            buf((STEPS * 16, part), BF16),
            buf((8, 128, HEAD_DIM), BF16),
            buf((8, 128, HEAD_DIM), BF16),
            buf((NX, STEPS, 16, 128), F32),
            buf((STRIDE, BLOCK, WIDE), BF16),
            buf((CHUNKS, CLASSES, SLAB, WIDE), BF16),
            buf((CHUNKS, CLASSES, SLAB, WIDE), BF16),
            buf((CHUNKS, peers, SLAB, WIDE), BF16),
            buf((NX, part, 2 * HIDE), BF16),
            buf((NX * HIDE, part), BF16),
            buf((CHUNKS, ROWS, 2 * HIDE), F32),
            buf((CHUNKS, NX, ROWS, 2 * HIDE), BF16),
            buf((CHUNKS, NX, ROWS, 2 * HIDE), BF16),
            buf((CHUNKS, NX, ROWS, HIDE), BF16),
            buf((CHUNKS, peers, SLAB, WIDE), BF16),
            buf((CHUNKS, peers, SLAB, WIDE), BF16),
            buf((STRIDE, PACK, WIDE), F32),
            buf((CHUNKS, CLASSES, SLAB, WIDE), BF16),
            buf((CHUNKS, CLASSES, SLAB, WIDE), BF16),
            buf((STRIDE, PACK, WIDE), BF16),
            buf((STRIDE, PACK, WIDE), BF16),
            sem((6,)),
            sem((15,)),
            sem((2,)),
            sem((2, NX)),
            sem((2, NX, 2)),
            sem((2, 8)),
            sem((2, CHUNKS, peers)),
            sem((2, CHUNKS, NX)),
            sem((2, CHUNKS, NX)),
            sem((2, CHUNKS, peers)),
            sem((2, 5)),
            sem((2, STRIDE)),
        ],
        compiler_params=pltpu.CompilerParams(
            collective_id=0, has_side_effects=True, vmem_limit_bytes=63 * 1024 * 1024
        ),
    )(*operands)
    return attn, moe


def solution(mesh):
    return jax.shard_map(
        local,
        mesh=mesh,
        in_specs=(
            P(None, "dp", "rep"),
            P(None, "dp", "rep"),
            P(None, "dp", "rep"),
            P(),
            P(),
            P("dp", None, None, "rep"),
            P("dp", None),
            P("dp"),
            P("dp"),
            P("dp"),
            P(None, "dp", "rep"),
            P(),
            P(None, "dp", None),
            P(None, "dp", None),
            P("dp", None, "rep"),
            P("dp", None, "rep"),
            P("dp", None, "rep"),
        ),
        out_specs=(P(None, "dp", "rep"), P(None, "dp", "rep")),
        check_vma=False,
    )
```
